256 devices in a mesh: inst: 32 (over x, y, core), tp: 8 (over z).
Axes of the slice: x: 4, y: 4, z: 8, core: 2. Of those that a mesh axis runs over, the one named last changes fastest.
Arguments:
- queries: bfloat16 [32, 8192], P('inst', 'tp'), may hold values from -8 to 8
- cache_keys: bfloat16 [64, 8, 4096, 128], P('inst', 'tp'), may hold values from -8 to 8
- cache_values: bfloat16 [64, 8, 4096, 128], P('inst', 'tp'), may hold values from -6 to 6
- block_request: int32 [64], replicated, may hold values from 0 to 7, as said below
- block_fill: int32 [64], replicated, may hold values from 1 to 4096
- out_weight: bfloat16 [8192, 4096], P('tp'), may hold values from -0.25 to 0.25
Outputs:
- mixed: bfloat16 [32, 4096], P('inst', 'tp')
The draws below stay inside these ranges and needn't reach their ends.
Inputs may be any that keep to these rules, and one draw needn't show every extreme that they name: `block_request`: every request 0 to 7 has at least one stored block.
All inputs are finite; a program needn't handle non-finite values.
Results may differ from the reference program's by a relative error of at most 0.0075.
Values may be sent and summed in bfloat16 or wider, within the bound.
A program may use at most 64 MiB of HBM per device.

```python
import jax
import jax.numpy as jnp
from jax import lax

HQ = 64
KVH = 8
HD = 128
DOUT = 4096
BLOCK = 4096
STEPS = 4
NB = 64
REQ = 8


def draw_queries(key, part):
    key = jax.random.fold_in(key, 3)
    key_normal = jax.random.fold_in(key, 0)
    base = 2.0 * jax.random.normal(key_normal, (REQ, STEPS, HQ, HD), jnp.float32)
    return jnp.clip(base, -8.0, 8.0).reshape(REQ * STEPS, HQ * HD).astype(jnp.bfloat16)


def draw_cache_keys(key, part):
    key = jax.random.fold_in(key, 5)
    base = jnp.clip(jax.random.normal(key, (NB, KVH, BLOCK, HD), jnp.float32), -6.0, 6.0)
    return base.astype(jnp.bfloat16)


def draw_block_request(key, part):
    key = jax.random.fold_in(key, 7)
    key_order, key_first, key_second, key_label = jax.random.split(key, 4)
    order = jax.random.permutation(key_order, NB)
    ranks = jnp.zeros((NB,), jnp.int32).at[order].set(jnp.arange(NB, dtype=jnp.int32))
    first_pick = jax.random.randint(key_first, (NB,), 0, REQ)
    second_pick = jax.random.randint(key_second, (NB,), 0, REQ)
    relabel = jax.random.permutation(key_label, REQ).astype(jnp.int32)
    skewed = relabel[jnp.minimum(first_pick, second_pick)]
    return jnp.where(ranks < REQ, ranks, skewed).astype(jnp.int32)


def draw_block_fill(key, part):
    key = jax.random.fold_in(key, 9)
    key_coin, key_count, key_place = jax.random.split(key, 3)
    coins = jax.random.randint(key_coin, (NB,), 0, 2)
    counts = jax.random.randint(key_count, (NB,), 1, BLOCK + 1)
    filled = jnp.where(coins == 1, BLOCK, counts)
    place = jax.random.randint(key_place, (), 0, NB)
    return filled.at[place].set(1).astype(jnp.int32)


def block_scale(rng, dims, shards, smallest, largest):
    def one(axis_at, shards_of):
        heights = jax.random.uniform(jax.random.fold_in(jax.random.fold_in(rng, 6), axis_at), (shards_of,), jnp.float32, smallest / len(shards), largest / len(shards))
        return jnp.repeat(jnp.exp(heights), dims[axis_at] // shards_of).reshape((-1,) + (1,) * (len(dims) - axis_at - 1))

    factor_of = one(*shards[0])
    for cut in shards[1:]:
        factor_of = factor_of * one(*cut)
    return factor_of


def noise(stream_key, extent, deviation, limit, shards=(), held_as=jnp.bfloat16):
    factor_of = block_scale(stream_key, extent, shards, -0.22, 0.18) if shards else 1.0
    array = jax.random.normal(stream_key, extent, jnp.float32) * deviation * factor_of
    return jnp.minimum(jnp.maximum(array, -limit), limit).astype(held_as)


def setup_inputs(seed: int = 0) -> dict:
    keys = jax.random.split(jax.random.key(seed), 7)
    return {
        "queries": draw_queries(jax.random.fold_in(keys[6], 71), 0),
        "cache_keys": draw_cache_keys(jax.random.fold_in(keys[6], 71), 0),
        "cache_values": noise(keys[2], (NB, KVH, BLOCK, HD), 1.0, 6.0, ((0, 32), (1, 8))),
        "block_request": draw_block_request(jax.random.fold_in(keys[6], 71), 0),
        "block_fill": draw_block_fill(jax.random.fold_in(keys[6], 71), 0),
        "out_weight": noise(keys[5], (HQ * HD, DOUT), (HQ * HD // 16) ** -0.5, 0.25, ((0, 8),)),
    }


NEGATIVE_FILL = -1e30


def block_partials(query_rows, key_block, value_block, fill_count):
    kv_heads = key_block.shape[0]
    group_size = HQ // KVH
    query_block = query_rows.reshape(STEPS, kv_heads, group_size, HD).transpose(1, 0, 2, 3).reshape(kv_heads, STEPS * group_size, HD)
    scores = jnp.einsum("kqd,ktd->kqt", query_block.astype(jnp.float32), key_block.astype(jnp.float32)) * (HD ** -0.5)
    valid_mask = jnp.arange(BLOCK, dtype=jnp.int32) < fill_count
    scores = jnp.where(valid_mask[None, None, :], scores, NEGATIVE_FILL)
    maxima = jnp.max(scores, axis=-1)
    probabilities = jnp.exp(scores - maxima[..., None]).astype(jnp.bfloat16)
    totals = jnp.sum(probabilities.astype(jnp.float32), axis=-1)
    outputs = jnp.einsum("kqt,ktd->kqd", probabilities.astype(jnp.float32), value_block.astype(jnp.float32))
    maxima = maxima.reshape(kv_heads, STEPS, group_size).transpose(1, 0, 2).reshape(STEPS, HQ)
    totals = totals.reshape(kv_heads, STEPS, group_size).transpose(1, 0, 2).reshape(STEPS, HQ)
    outputs = outputs.reshape(kv_heads, STEPS, group_size, HD).transpose(1, 0, 2, 3).reshape(STEPS, HQ, HD)
    return maxima, totals, outputs


def reference(queries, cache_keys, cache_values, block_request, block_fill, out_weight):
    query_table = queries.reshape(REQ, STEPS, HQ * HD)

    def partial_of_block(block_index):
        request_id = block_request[block_index]
        query_rows = lax.dynamic_index_in_dim(query_table, request_id, 0, keepdims=False)
        return block_partials(query_rows, cache_keys[block_index], cache_values[block_index], block_fill[block_index])

    maxima, totals, outputs = lax.map(partial_of_block, jnp.arange(NB, dtype=jnp.int32))
    owners = jnp.arange(REQ, dtype=jnp.int32)
    matches = (block_request[None, :] == owners[:, None])[:, :, None, None]
    best_top = jnp.max(jnp.where(matches, maxima[None], NEGATIVE_FILL), axis=1)
    weights = jnp.where(matches, jnp.exp(jnp.minimum(maxima[None] - best_top[:, None], 0.0)), 0.0)
    sums_total = jnp.sum(weights * totals[None], axis=1)
    merged = jnp.einsum("rbsh,bshd->rshd", weights, outputs, precision=lax.Precision.HIGHEST)
    attention = (merged / sums_total[..., None]).reshape(REQ * STEPS, HQ * HD).astype(jnp.bfloat16)
    mixed = jnp.dot(attention, out_weight, preferred_element_type=jnp.float32)
    return mixed.astype(jnp.bfloat16)
```

```python
import math

import jax
import jax.numpy as jnp
from jax import lax
from jax.experimental import pallas as pl
from jax.experimental.pallas import tpu as pltpu
from jax.sharding import PartitionSpec as P

MESH = pl.DeviceIdType.MESH
EMPTY = -1e30


def kernel(
    n_inst,
    n_tp,
    req_ref,
    fill_ref,
    q_ref,
    k_hbm,
    v_hbm,
    w_hbm,
    out_ref,
    kbuf,
    vbuf,
    wbuf,
    q_all,
    msg,
    got,
    part,
    parts,
    local_sem,
    q_send,
    q_recv,
    m_send,
    m_recv,
    p_send,
    p_recv,
):
    me = lax.axis_index("inst")
    my_tp = lax.axis_index("tp")
    blocks, block_len, head_size = kbuf.shape
    heads = q_all.shape[1]
    steps = 4
    rows = steps * heads
    requests = n_inst // steps
    out_cols = out_ref.shape[1]
    scale = head_size**-0.5 * math.log2(math.e)

    k_copies = [
        pltpu.make_async_copy(k_hbm.at[b, 0], kbuf.at[b], local_sem.at[b]) for b in range(blocks)
    ]
    v_copies = [
        pltpu.make_async_copy(v_hbm.at[b, 0], vbuf.at[b], local_sem.at[blocks + b])
        for b in range(blocks)
    ]
    w_copy = pltpu.make_async_copy(w_hbm, wbuf, local_sem.at[2 * blocks])
    for c in k_copies + v_copies + [w_copy]:
        c.start()

    barrier = pltpu.get_barrier_semaphore()

    def greet_inst(i, _):
        pl.semaphore_signal(
            barrier, inc=1, device_id={"inst": lax.rem(me + i, n_inst)}, device_id_type=MESH
        )
        return 0

    def greet_tp(i, _):
        pl.semaphore_signal(
            barrier, inc=1, device_id={"tp": lax.rem(my_tp + i, n_tp)}, device_id_type=MESH
        )
        return 0

    lax.fori_loop(1, n_inst, greet_inst, 0)
    lax.fori_loop(1, n_tp, greet_tp, 0)

    for h in range(heads):
        q_all[me, h : h + 1, :] = q_ref[:, h * head_size : (h + 1) * head_size].astype(jnp.float32)

    pl.semaphore_wait(barrier, n_inst + n_tp - 2)

    def send_q(i, _):
        pltpu.make_async_remote_copy(
            src_ref=q_all.at[me],
            dst_ref=q_all.at[me],
            send_sem=q_send,
            recv_sem=q_recv,
            device_id={"inst": lax.rem(me + i, n_inst)},
            device_id_type=MESH,
        ).start()
        return 0

    lax.fori_loop(1, n_inst, send_q, 0)
    others = q_all.at[pl.ds(0, n_inst - 1)]
    pltpu.make_async_copy(others, others, q_recv).wait()
    pltpu.make_async_copy(others, others, q_send).wait()

    tops, totals, outs, owners = [], [], [], []
    for b in range(blocks):
        request = req_ref[me * blocks + b]
        fill = fill_ref[me * blocks + b]
        q = q_all[pl.ds(request * steps, steps)].reshape(rows, head_size).astype(jnp.bfloat16)
        k_copies[b].wait()
        s = lax.dot_general(
            q, kbuf[b], (((1,), (1,)), ((), ())), preferred_element_type=jnp.float32
        )
        used = lax.broadcasted_iota(jnp.int32, s.shape, 1) < fill
        s = jnp.where(used, s * scale, EMPTY)
        top = jnp.max(s, axis=1, keepdims=True).astype(jnp.bfloat16).astype(jnp.float32)
        p = jnp.exp2(s - top)
        total = jnp.sum(p, axis=1, keepdims=True)
        v_copies[b].wait()
        o = jnp.dot(p.astype(jnp.bfloat16), vbuf[b], preferred_element_type=jnp.float32)
        tops.append(top)
        totals.append(total)
        outs.append(o)
        owners.append(request)

    lane = lax.broadcasted_iota(jnp.int32, (rows, head_size), 1)

    def pack(top, total, o):
        o = o / total
        high = total.astype(jnp.bfloat16).astype(jnp.float32)
        stats = jnp.where(lane == 0, top, jnp.where(lane == 1, high, total - high))
        o = o.reshape(steps, heads, head_size)
        stats = stats.reshape(steps, heads, head_size)
        return jnp.concatenate([o, stats], axis=1)

    both_top = jnp.maximum(tops[0], tops[1])
    w0 = jnp.exp2(tops[0] - both_top)
    w1 = jnp.exp2(tops[1] - both_top)
    both = pack(both_top, w0 * totals[0] + w1 * totals[1], w0 * outs[0] + w1 * outs[1])
    same = owners[0] == owners[1]
    first = jnp.where(same, both, pack(tops[0], totals[0], outs[0]))
    second = jnp.where(same, both, pack(tops[1], totals[1], outs[1]))
    row = lax.broadcasted_iota(jnp.int32, first.shape, 1)
    lanes = lax.broadcasted_iota(jnp.int32, first.shape, 2)
    empty = jnp.where((row >= heads) & (lanes == 0), EMPTY, 0.0)
    for r in range(requests):
        tile = jnp.where(owners[0] == r, first, jnp.where(owners[1] == r, second, empty))
        msg[r * steps : (r + 1) * steps] = tile.astype(jnp.bfloat16)
    got[me] = msg[me]

    def send_m(i, _):
        peer = lax.rem(me + i, n_inst)
        pltpu.make_async_remote_copy(
            src_ref=msg.at[peer],
            dst_ref=got.at[me],
            send_sem=m_send,
            recv_sem=m_recv,
            device_id={"inst": peer},
            device_id_type=MESH,
        ).start()
        return 0

    lax.fori_loop(1, n_inst, send_m, 0)
    others = got.at[pl.ds(0, n_inst - 1)]
    pltpu.make_async_copy(others, others, m_recv).wait()
    pltpu.make_async_copy(others, others, m_send).wait()

    tile = got[...].astype(jnp.float32)
    o = tile[:, :heads]
    top = tile[:, heads:, 0:1]
    total = tile[:, heads:, 1:2] + tile[:, heads:, 2:3]
    best = jnp.max(top, axis=0, keepdims=True)
    weight = jnp.exp2(top - best) * total
    att = jnp.sum(weight * o, axis=0) / jnp.sum(weight, axis=0)
    att = jnp.concatenate([att[h : h + 1] for h in range(heads)], axis=1).astype(jnp.bfloat16)

    w_copy.wait()

    def project(i, _):
        peer = lax.rem(my_tp + i, n_tp)
        cols = pl.ds(pl.multiple_of(peer * out_cols, out_cols), out_cols)
        part[peer] = jnp.dot(att, wbuf[:, cols], preferred_element_type=jnp.float32)
        pltpu.make_async_remote_copy(
            src_ref=part.at[peer],
            dst_ref=parts.at[my_tp],
            send_sem=p_send,
            recv_sem=p_recv,
            device_id={"tp": peer},
            device_id_type=MESH,
        ).start()
        return 0

    lax.fori_loop(1, n_tp, project, 0)
    cols = pl.ds(pl.multiple_of(my_tp * out_cols, out_cols), out_cols)
    parts[my_tp] = jnp.dot(att, wbuf[:, cols], preferred_element_type=jnp.float32)
    others = parts.at[pl.ds(0, n_tp - 1)]
    pltpu.make_async_copy(others, others, p_recv).wait()
    pltpu.make_async_copy(others, others, p_send).wait()
    out_ref[...] = jnp.sum(parts[...], axis=0).astype(out_ref.dtype)


def solution(mesh):
    n_inst, n_tp = mesh.shape["inst"], mesh.shape["tp"]

    def body(queries, cache_keys, cache_values, block_request, block_fill, out_weight):
        blocks, _, block_len, head_size = cache_keys.shape
        width, dout = out_weight.shape
        heads = width // head_size
        cols = dout // n_tp
        any_spec = pl.BlockSpec(memory_space=pl.ANY)
        smem_spec = pl.BlockSpec(memory_space=pltpu.SMEM)
        vmem_spec = pl.BlockSpec(memory_space=pltpu.VMEM)
        dma = pltpu.SemaphoreType.DMA
        return pl.pallas_call(
            lambda *refs: kernel(n_inst, n_tp, *refs),
            out_shape=jax.ShapeDtypeStruct((1, cols), jnp.bfloat16),
            in_specs=[smem_spec, smem_spec, vmem_spec, any_spec, any_spec, any_spec],
            out_specs=vmem_spec,
            scratch_shapes=[
                pltpu.VMEM((blocks, block_len, head_size), jnp.bfloat16),
                pltpu.VMEM((blocks, block_len, head_size), jnp.bfloat16),
                pltpu.VMEM((width, dout), jnp.bfloat16),
                pltpu.VMEM((n_inst, heads, head_size), jnp.float32),
                pltpu.VMEM((n_inst, 2 * heads, head_size), jnp.bfloat16),
                pltpu.VMEM((n_inst, 2 * heads, head_size), jnp.bfloat16),
                pltpu.VMEM((n_tp, 1, cols), jnp.float32),
                pltpu.VMEM((n_tp, 1, cols), jnp.float32),
                dma((2 * blocks + 1,)),
                dma,
                dma,
                dma,
                dma,
                dma,
                dma,
            ],
            compiler_params=pltpu.CompilerParams(
                collective_id=0, has_side_effects=True, vmem_limit_bytes=60 * 1024 * 1024
            ),
            name="paged_decode",
        )(block_request, block_fill, queries, cache_keys, cache_values, out_weight)

    in_specs = (
        P("inst", "tp"),
        P("inst", "tp", None, None),
        P("inst", "tp", None, None),
        P(),
        P(),
        P("tp", None),
    )
    return jax.shard_map(
        body, mesh=mesh, in_specs=in_specs, out_specs=P("inst", "tp"), check_vma=False
    )
```

```python
import math

import jax
import jax.numpy as jnp
from jax import lax
from jax.experimental import pallas as pl
from jax.experimental.pallas import tpu as pltpu
from jax.sharding import PartitionSpec as P

MESH = pl.DeviceIdType.MESH
EMPTY = -1e30
STEPS = 4
SIDE = 4


def ring(d, n):
    return min(d, n - d)


PLANE = sorted(
    [(x, y, c) for x in range(SIDE) for y in range(SIDE) for c in range(2)][1:],
    key=lambda d: -(ring(d[0], SIDE) + ring(d[1], SIDE) + 0.5 * d[2]),
)


def kernel(
    n_tp,
    req_hbm,
    fill_hbm,
    q_hbm,
    k_hbm,
    v_hbm,
    w_hbm,
    out_hbm,
    req_ref,
    fill_ref,
    q_in,
    kbuf,
    kt,
    vbuf,
    wbuf,
    q_all,
    msg,
    got,
    part,
    local_sem,
    q_send,
    q_recv,
    m_send,
    m_recv,
    p_send,
    p_recv,
):
    me = lax.axis_index("inst")
    my_tp = lax.axis_index("tp")
    blocks, block_len, head_size = kbuf.shape
    n_inst, heads, _ = q_all.shape
    rows = STEPS * heads
    requests = n_inst // STEPS
    out_cols = part.shape[2]
    scale = head_size**-0.5 * math.log2(math.e)
    f32, bf16 = jnp.float32, jnp.bfloat16

    my_x, my_y, my_core = me // (2 * SIDE), (me // 2) % SIDE, me % 2
    plane = [
        (((my_x + x) % SIDE) * SIDE + (my_y + y) % SIDE) * 2 + (my_core + c) % 2
        for x, y, c in PLANE
    ]
    z_ring = [
        (my_tp + d) % n_tp for d in sorted(range(1, n_tp), key=lambda d: -ring(d, n_tp))
    ]

    barrier = pltpu.get_barrier_semaphore()
    for peer in plane:
        pl.semaphore_signal(barrier, inc=1, device_id={"inst": peer}, device_id_type=MESH)
    for peer in z_ring:
        pl.semaphore_signal(barrier, inc=1, device_id={"tp": peer}, device_id_type=MESH)

    q_copy = pltpu.make_async_copy(q_hbm, q_in, local_sem.at[0])
    req_copy = pltpu.make_async_copy(req_hbm, req_ref, local_sem.at[1])
    fill_copy = pltpu.make_async_copy(fill_hbm, fill_ref, local_sem.at[2])
    k_copy = pltpu.make_async_copy(k_hbm.at[:, 0], kbuf, local_sem.at[3])
    v_copies = [
        pltpu.make_async_copy(
            v_hbm.at[b, 0],
            vbuf.at[:, pl.ds(b * head_size, head_size)],
            local_sem.at[4 + b],
        )
        for b in range(blocks)
    ]
    w_copy = pltpu.make_async_copy(w_hbm, wbuf, local_sem.at[4 + blocks])
    for c in [q_copy, k_copy, req_copy, fill_copy] + v_copies + [w_copy]:
        c.start()
    q_copy.wait()
    for h in range(heads):
        q_all[me, h : h + 1, :] = q_in[:, h * head_size : (h + 1) * head_size].astype(f32)
    pl.semaphore_wait(barrier, len(plane) + len(z_ring))

    for peer in plane:
        pltpu.make_async_remote_copy(
            src_ref=q_all.at[me],
            dst_ref=q_all.at[me],
            send_sem=q_send,
            recv_sem=q_recv,
            device_id={"inst": peer},
            device_id_type=MESH,
        ).start()

    k_copy.wait()
    for b in range(blocks):
        kt[b * head_size : (b + 1) * head_size, :] = kbuf[b].T
    req_copy.wait()
    fill_copy.wait()
    for c in v_copies:
        c.wait()
    request = [req_ref[me * blocks + b] for b in range(blocks)]
    fill = [fill_ref[me * blocks + b] for b in range(blocks)]

    q_others = q_all.at[pl.ds(0, n_inst - 1)]
    pltpu.make_async_copy(q_others, q_others, q_recv).wait()

    q = [q_all[pl.ds(r * STEPS, STEPS)].reshape(rows, head_size).astype(bf16) for r in request]
    zero = jnp.zeros_like(q[0])
    q = jnp.concatenate(
        [jnp.concatenate([q[0], zero], axis=1), jnp.concatenate([zero, q[1]], axis=1)], axis=0
    )
    s = jnp.dot(q, kt[...], preferred_element_type=f32)
    slot = lax.broadcasted_iota(jnp.int32, (rows, block_len), 1)
    s = jnp.concatenate(
        [jnp.where(slot < fill[b], s[b * rows : (b + 1) * rows], EMPTY) for b in range(blocks)],
        axis=0,
    )
    top = (jnp.max(s, axis=1, keepdims=True) * scale).astype(bf16).astype(f32)
    p = jnp.exp2(s * scale - top)
    total = jnp.sum(p, axis=1, keepdims=True)
    o = jnp.dot(p.astype(bf16), vbuf[...], preferred_element_type=f32)
    tops = [top[:rows], top[rows:]]
    totals = [total[:rows], total[rows:]]
    outs = [o[:rows, :head_size], o[rows:, head_size:]]

    lane = lax.broadcasted_iota(jnp.int32, (rows, head_size), 1)

    def pack(top, total, o):
        o = o * (1.0 / total)
        high = total.astype(bf16).astype(f32)
        stats = jnp.where(lane == 0, top, jnp.where(lane == 1, high, total - high))
        o = o.reshape(STEPS, heads, head_size)
        stats = stats.reshape(STEPS, heads, head_size)
        return jnp.concatenate([o, stats], axis=1).astype(bf16)

    both_top = jnp.maximum(tops[0], tops[1])
    w0 = jnp.exp2(tops[0] - both_top)
    w1 = jnp.exp2(tops[1] - both_top)
    both = pack(both_top, w0 * totals[0] + w1 * totals[1], w0 * outs[0] + w1 * outs[1])
    same = request[0] == request[1]
    first = jnp.where(same, both, pack(tops[0], totals[0], outs[0]))
    second = jnp.where(same, both, pack(tops[1], totals[1], outs[1]))
    row = lax.broadcasted_iota(jnp.int32, (STEPS, 2 * heads, head_size), 1)
    lanes = lax.broadcasted_iota(jnp.int32, (STEPS, 2 * heads, head_size), 2)
    empty = jnp.where((row >= heads) & (lanes == 0), EMPTY, 0.0).astype(bf16)
    for r in range(requests):
        msg[r * STEPS : (r + 1) * STEPS] = jnp.where(
            request[0] == r, first, jnp.where(request[1] == r, second, empty)
        )
    for peer in plane:
        pltpu.make_async_remote_copy(
            src_ref=msg.at[peer],
            dst_ref=got.at[me],
            send_sem=m_send,
            recv_sem=m_recv,
            device_id={"inst": peer},
            device_id_type=MESH,
        ).start()
    got[me] = msg[me]
    w_copy.wait()
    m_others = got.at[pl.ds(0, n_inst - 1)]
    pltpu.make_async_copy(m_others, m_others, m_recv).wait()

    tile = got[...].astype(f32)
    o = tile[:, :heads]
    top = tile[:, heads:, 0:1]
    total = tile[:, heads:, 1:2] + tile[:, heads:, 2:3]
    best = jnp.max(top, axis=0, keepdims=True)
    weight = jnp.exp2(top - best) * total
    att = jnp.sum(weight * o, axis=0) / jnp.sum(weight, axis=0)
    att = jnp.concatenate([att[h : h + 1] for h in range(heads)], axis=1).astype(bf16)

    for peer in z_ring + [my_tp]:
        cols = pl.ds(pl.multiple_of(peer * out_cols, out_cols), out_cols)
        part[peer] = jnp.dot(att, wbuf[:, cols], preferred_element_type=f32)
        if peer is not my_tp:
            pltpu.make_async_remote_copy(
                src_ref=part.at[peer],
                dst_ref=out_hbm.at[my_tp],
                send_sem=p_send,
                recv_sem=p_recv,
                device_id={"tp": peer},
                device_id_type=MESH,
            ).start()
    own = pltpu.make_async_copy(part.at[my_tp], out_hbm.at[my_tp], local_sem.at[0])
    own.start()
    pltpu.make_async_copy(q_others, q_others, q_send).wait()
    pltpu.make_async_copy(m_others, m_others, m_send).wait()
    p_others = part.at[pl.ds(0, n_tp - 1)]
    pltpu.make_async_copy(p_others, p_others, p_send).wait()
    own.wait()
    p_others = out_hbm.at[pl.ds(0, n_tp - 1)]
    pltpu.make_async_copy(p_others, p_others, p_recv).wait()


def add_up(parts_ref, out_ref):
    out_ref[...] = jnp.sum(parts_ref[...], axis=0).astype(out_ref.dtype)


def solution(mesh):
    n_inst, n_tp = mesh.shape["inst"], mesh.shape["tp"]

    def body(queries, cache_keys, cache_values, block_request, block_fill, out_weight):
        blocks, _, block_len, head_size = cache_keys.shape
        width, dout = out_weight.shape
        heads = width // head_size
        cols = dout // n_tp
        any_spec = pl.BlockSpec(memory_space=pl.ANY)
        dma = pltpu.SemaphoreType.DMA
        bf16, f32 = jnp.bfloat16, jnp.float32
        parts = pl.pallas_call(
            lambda *refs: kernel(n_tp, *refs),
            out_shape=jax.ShapeDtypeStruct((n_tp, 1, cols), f32),
            in_specs=[any_spec] * 6,
            out_specs=any_spec,
            scratch_shapes=[
                pltpu.SMEM(block_request.shape, jnp.int32),
                pltpu.SMEM(block_fill.shape, jnp.int32),
                pltpu.VMEM(queries.shape, bf16),
                pltpu.VMEM((blocks, block_len, head_size), bf16),
                pltpu.VMEM((blocks * head_size, block_len), bf16),
                pltpu.VMEM((block_len, blocks * head_size), bf16),
                pltpu.VMEM((width, dout), bf16),
                pltpu.VMEM((n_inst, heads, head_size), f32),
                pltpu.VMEM((n_inst, 2 * heads, head_size), bf16),
                pltpu.VMEM((n_inst, 2 * heads, head_size), bf16),
                pltpu.VMEM((n_tp, 1, cols), f32),
                dma((5 + blocks,)),
                dma,
                dma,
                dma,
                dma,
                dma,
                dma,
            ],
            compiler_params=pltpu.CompilerParams(
                collective_id=0, has_side_effects=True, vmem_limit_bytes=60 * 1024 * 1024
            ),
            name="paged_decode",
        )(block_request, block_fill, queries, cache_keys, cache_values, out_weight)
        return pl.pallas_call(
            add_up,
            out_shape=jax.ShapeDtypeStruct((1, cols), bf16),
            name="add_up",
        )(parts)

    in_specs = (
        P("inst", "tp"),
        P("inst", "tp", None, None),
        P("inst", "tp", None, None),
        P(),
        P(),
        P("tp", None),
    )
    return jax.shard_map(
        body, mesh=mesh, in_specs=in_specs, out_specs=P("inst", "tp"), check_vma=False
    )
```

```python
import math

import jax
import jax.numpy as jnp
from jax import lax
from jax.experimental import pallas as pl
from jax.experimental.pallas import tpu as pltpu
from jax.sharding import PartitionSpec as P

MESH = pl.DeviceIdType.MESH
EMPTY = -1e30
STEPS = 4
SIDE = 4


def ring(d, n):
    return min(d, n - d)


PLANE = sorted(
    [(x, y, c) for x in range(SIDE) for y in range(SIDE) for c in range(2)][1:],
    key=lambda d: -(ring(d[0], SIDE) + ring(d[1], SIDE) + 0.5 * d[2]),
)


def kernel(
    n_tp,
    req_hbm,
    fill_hbm,
    q_hbm,
    k_hbm,
    v_hbm,
    w_hbm,
    out_ref,
    req_ref,
    fill_ref,
    q_in,
    kbuf,
    kt,
    vbuf,
    wbuf,
    q_all,
    msg,
    got,
    part,
    parts,
    local_sem,
    q_send,
    q_recv,
    m_send,
    m_recv,
    p_send,
    p_recv,
):
    me = lax.axis_index("inst")
    my_tp = lax.axis_index("tp")
    blocks, block_len, head_size = kbuf.shape
    n_inst, heads, _ = q_all.shape
    rows = STEPS * heads
    requests = n_inst // STEPS
    out_cols = part.shape[2]
    scale = head_size**-0.5 * math.log2(math.e)
    f32, bf16 = jnp.float32, jnp.bfloat16

    my_x, my_y, my_core = me // (2 * SIDE), (me // 2) % SIDE, me % 2
    plane = [
        (((my_x + x) % SIDE) * SIDE + (my_y + y) % SIDE) * 2 + (my_core + c) % 2
        for x, y, c in PLANE
    ]
    z_ring = [
        (my_tp + d) % n_tp for d in sorted(range(1, n_tp), key=lambda d: -ring(d, n_tp))
    ]

    barrier = pltpu.get_barrier_semaphore()
    for peer in plane:
        pl.semaphore_signal(barrier, inc=1, device_id={"inst": peer}, device_id_type=MESH)
    for peer in z_ring:
        pl.semaphore_signal(barrier, inc=1, device_id={"tp": peer}, device_id_type=MESH)

    q_copy = pltpu.make_async_copy(q_hbm, q_in, local_sem.at[0])
    req_copy = pltpu.make_async_copy(req_hbm, req_ref, local_sem.at[1])
    fill_copy = pltpu.make_async_copy(fill_hbm, fill_ref, local_sem.at[2])
    k_copy = pltpu.make_async_copy(k_hbm.at[:, 0], kbuf, local_sem.at[3])
    v_copy = pltpu.make_async_copy(v_hbm.at[:, 0], vbuf, local_sem.at[4])
    w_copy = pltpu.make_async_copy(w_hbm, wbuf, local_sem.at[5])
    for c in [q_copy, k_copy, req_copy, fill_copy, v_copy, w_copy]:
        c.start()
    q_copy.wait()
    for h in range(heads):
        q_all[me, h : h + 1, :] = q_in[:, h * head_size : (h + 1) * head_size].astype(f32)
    pl.semaphore_wait(barrier, len(plane) + len(z_ring))

    for peer in plane:
        pltpu.make_async_remote_copy(
            src_ref=q_all.at[me],
            dst_ref=q_all.at[me],
            send_sem=q_send,
            recv_sem=q_recv,
            device_id={"inst": peer},
            device_id_type=MESH,
        ).start()

    k_copy.wait()
    for b in range(blocks):
        kt[b] = kbuf[b].T
    req_copy.wait()
    fill_copy.wait()
    v_copy.wait()
    request = [req_ref[me * blocks + b] for b in range(blocks)]
    fill = [fill_ref[me * blocks + b] for b in range(blocks)]

    q_others = q_all.at[pl.ds(0, n_inst - 1)]
    pltpu.make_async_copy(q_others, q_others, q_recv).wait()

    scores = []
    for b in range(blocks):
        q = q_all[pl.ds(request[b] * STEPS, STEPS)].reshape(rows, head_size).astype(bf16)
        scores.append(jnp.dot(q, kt[b], preferred_element_type=f32))
    tops, totals, outs = [], [], []
    for b in range(blocks):
        slot = lax.broadcasted_iota(jnp.int32, (rows, block_len), 1)
        s = jnp.where(slot < fill[b], scores[b], EMPTY)
        top = (jnp.max(s, axis=1, keepdims=True) * scale).astype(bf16).astype(f32)
        p = jnp.exp2(s * scale - top)
        tops.append(top)
        totals.append(jnp.sum(p, axis=1, keepdims=True))
        outs.append(jnp.dot(p.astype(bf16), vbuf[b], preferred_element_type=f32))

    lane = lax.broadcasted_iota(jnp.int32, (rows, head_size), 1)

    def pack(top, total, o):
        o = o * (1.0 / total)
        high = total.astype(bf16).astype(f32)
        stats = jnp.where(lane == 0, top, jnp.where(lane == 1, high, total - high))
        o = o.reshape(STEPS, heads, head_size)
        stats = stats.reshape(STEPS, heads, head_size)
        return jnp.concatenate([o, stats], axis=1).astype(bf16)

    both_top = jnp.maximum(tops[0], tops[1])
    w0 = jnp.exp2(tops[0] - both_top)
    w1 = jnp.exp2(tops[1] - both_top)
    both = pack(both_top, w0 * totals[0] + w1 * totals[1], w0 * outs[0] + w1 * outs[1])
    same = request[0] == request[1]
    first = jnp.where(same, both, pack(tops[0], totals[0], outs[0]))
    second = jnp.where(same, both, pack(tops[1], totals[1], outs[1]))
    row = lax.broadcasted_iota(jnp.int32, (STEPS, 2 * heads, head_size), 1)
    lanes = lax.broadcasted_iota(jnp.int32, (STEPS, 2 * heads, head_size), 2)
    empty = jnp.where((row >= heads) & (lanes == 0), EMPTY, 0.0).astype(bf16)
    for r in range(requests):
        msg[r * STEPS : (r + 1) * STEPS] = jnp.where(
            request[0] == r, first, jnp.where(request[1] == r, second, empty)
        )
    for peer in plane:
        pltpu.make_async_remote_copy(
            src_ref=msg.at[peer],
            dst_ref=got.at[me],
            send_sem=m_send,
            recv_sem=m_recv,
            device_id={"inst": peer},
            device_id_type=MESH,
        ).start()
    got[me] = msg[me]
    w_copy.wait()
    m_others = got.at[pl.ds(0, n_inst - 1)]
    pltpu.make_async_copy(m_others, m_others, m_recv).wait()

    tile = got[...].astype(f32)
    o = tile[:, :heads]
    top = tile[:, heads:, 0:1]
    total = tile[:, heads:, 1:2] + tile[:, heads:, 2:3]
    best = jnp.max(top, axis=0, keepdims=True)
    weight = jnp.exp2(top - best) * total
    att = jnp.sum(weight * o, axis=0) / jnp.sum(weight, axis=0)
    att = jnp.concatenate([att[h : h + 1] for h in range(heads)], axis=1).astype(bf16)

    for peer in z_ring + [my_tp]:
        cols = pl.ds(pl.multiple_of(peer * out_cols, out_cols), out_cols)
        part[peer] = jnp.dot(att, wbuf[:, cols], preferred_element_type=f32)
        if peer is not my_tp:
            pltpu.make_async_remote_copy(
                src_ref=part.at[peer],
                dst_ref=parts.at[my_tp],
                send_sem=p_send,
                recv_sem=p_recv,
                device_id={"tp": peer},
                device_id_type=MESH,
            ).start()
    parts[my_tp] = part[my_tp]
    pltpu.make_async_copy(q_others, q_others, q_send).wait()
    pltpu.make_async_copy(m_others, m_others, m_send).wait()
    p_others = parts.at[pl.ds(0, n_tp - 1)]
    pltpu.make_async_copy(p_others, p_others, p_send).wait()
    pltpu.make_async_copy(p_others, p_others, p_recv).wait()
    out_ref[...] = jnp.sum(parts[...], axis=0).astype(out_ref.dtype)


def solution(mesh):
    n_inst, n_tp = mesh.shape["inst"], mesh.shape["tp"]

    def body(queries, cache_keys, cache_values, block_request, block_fill, out_weight):
        blocks, _, block_len, head_size = cache_keys.shape
        width, dout = out_weight.shape
        heads = width // head_size
        cols = dout // n_tp
        any_spec = pl.BlockSpec(memory_space=pl.ANY)
        dma = pltpu.SemaphoreType.DMA
        bf16, f32 = jnp.bfloat16, jnp.float32
        operands = [
            pltpu.with_memory_space_constraint(a, pltpu.HBM)
            for a in (
                block_request,
                block_fill,
                queries,
                cache_keys,
                cache_values,
                out_weight,
            )
        ]
        return pl.pallas_call(
            lambda *refs: kernel(n_tp, *refs),
            out_shape=jax.ShapeDtypeStruct((1, cols), bf16),
            in_specs=[any_spec] * 6,
            out_specs=pl.BlockSpec(memory_space=pltpu.VMEM),
            scratch_shapes=[
                pltpu.SMEM(block_request.shape, jnp.int32),
                pltpu.SMEM(block_fill.shape, jnp.int32),
                pltpu.VMEM(queries.shape, bf16),
                pltpu.VMEM((blocks, block_len, head_size), bf16),
                pltpu.VMEM((blocks, head_size, block_len), bf16),
                pltpu.VMEM((blocks, block_len, head_size), bf16),
                pltpu.VMEM((width, dout), bf16),
                pltpu.VMEM((n_inst, heads, head_size), f32),
                pltpu.VMEM((n_inst, 2 * heads, head_size), bf16),
                pltpu.VMEM((n_inst, 2 * heads, head_size), bf16),
                pltpu.VMEM((n_tp, 1, cols), f32),
                pltpu.VMEM((n_tp, 1, cols), f32),
                dma((6,)),
                dma,
                dma,
                dma,
                dma,
                dma,
                dma,
            ],
            compiler_params=pltpu.CompilerParams(
                collective_id=0, has_side_effects=True, vmem_limit_bytes=40 * 1024 * 1024
            ),
            name="paged_decode",
        )(*operands)

    in_specs = (
        P("inst", "tp"),
        P("inst", "tp", None, None),
        P("inst", "tp", None, None),
        P(),
        P(),
        P("tp", None),
    )
    return jax.shard_map(
        body, mesh=mesh, in_specs=in_specs, out_specs=P("inst", "tp"), check_vma=False
    )
```

```python
import functools
import math

import jax
import jax.numpy as jnp
from jax import lax
from jax.experimental import pallas as pl
from jax.experimental.pallas import tpu as pltpu
from jax.sharding import PartitionSpec as P

MESH = pl.DeviceIdType.MESH
EMPTY = -1e30
STEPS = 4
SIDE = 4


def ring(d, n):
    return min(d, n - d)


CHIPS = sorted(
    [(x, y) for x in range(SIDE) for y in range(SIDE)][1:],
    key=lambda d: -(ring(d[0], SIDE) + ring(d[1], SIDE)),
)


def kernel(
    n_tp,
    req_hbm,
    fill_hbm,
    q_hbm,
    k_hbm,
    v_hbm,
    w_hbm,
    out_ref,
    req_ref,
    fill_ref,
    q_in,
    kbuf,
    kt,
    vbuf,
    wbuf,
    q_all,
    msg,
    got,
    part,
    parts,
    local_sem,
    q_send,
    q_recv,
    m_send,
    m_recv,
    p_send,
    p_recv,
):
    me = lax.axis_index("inst")
    my_tp = lax.axis_index("tp")
    blocks, block_len, head_size = kbuf.shape
    n_inst, heads, _ = q_all.shape
    rows = STEPS * heads
    requests = n_inst // STEPS
    out_cols = part.shape[2]
    scale = head_size**-0.5 * math.log2(math.e)
    f32, bf16 = jnp.float32, jnp.bfloat16

    my_x, my_y, my_core = me // (2 * SIDE), (me // 2) % SIDE, me % 2
    plane = []
    for x, y in CHIPS:
        chip = ((my_x + x) % SIDE) * SIDE + (my_y + y) % SIDE
        plane += [2 * chip, 2 * chip + 1]
    plane.append(me + 1 - 2 * my_core)
    z_ring = [
        (my_tp + d) % n_tp for d in sorted(range(1, n_tp), key=lambda d: -ring(d, n_tp))
    ]

    barrier = pltpu.get_barrier_semaphore()
    for peer in plane:
        pl.semaphore_signal(barrier, inc=1, device_id={"inst": peer}, device_id_type=MESH)
    for peer in z_ring:
        pl.semaphore_signal(barrier, inc=1, device_id={"tp": peer}, device_id_type=MESH)

    q_copy = pltpu.make_async_copy(q_hbm, q_in, local_sem.at[0])
    req_copy = pltpu.make_async_copy(req_hbm, req_ref, local_sem.at[1])
    fill_copy = pltpu.make_async_copy(fill_hbm, fill_ref, local_sem.at[2])
    k_copy = pltpu.make_async_copy(k_hbm.at[:, 0], kbuf, local_sem.at[3])
    v_copy = pltpu.make_async_copy(v_hbm.at[:, 0], vbuf, local_sem.at[4])
    w_copy = pltpu.make_async_copy(w_hbm, wbuf, local_sem.at[5])
    for c in [q_copy, k_copy, req_copy, fill_copy, v_copy]:
        c.start()
    q_copy.wait()
    own_q = q_in[...].astype(f32)
    q_all[me] = jnp.concatenate(
        [own_q[:, h * head_size : (h + 1) * head_size] for h in range(heads)], axis=0
    ).astype(bf16)
    pl.semaphore_wait(barrier, len(plane) + len(z_ring))

    for peer in plane:
        pltpu.make_async_remote_copy(
            src_ref=q_all.at[me],
            dst_ref=q_all.at[me],
            send_sem=q_send,
            recv_sem=q_recv,
            device_id={"inst": peer},
            device_id_type=MESH,
        ).start()

    w_copy.start()

    k_copy.wait()
    for b in range(blocks):
        kt[b] = kbuf[b].T
    req_copy.wait()
    fill_copy.wait()
    v_copy.wait()
    request = [req_ref[me * blocks + b] for b in range(blocks)]
    fill = [fill_ref[me * blocks + b] for b in range(blocks)]

    q_others = q_all.at[pl.ds(0, n_inst - 1)]
    pltpu.make_async_copy(q_others, q_others, q_recv).wait()

    scores = []
    for b in range(blocks):
        q = q_all[pl.ds(request[b] * STEPS, STEPS)].reshape(rows, head_size)
        scores.append(jnp.dot(q, kt[b], preferred_element_type=f32))
    tops, totals, outs = [], [], []
    for b in range(blocks):
        slot = lax.broadcasted_iota(jnp.int32, (rows, block_len), 1)
        s = jnp.where(slot < fill[b], scores[b], EMPTY)
        top = (jnp.max(s, axis=1, keepdims=True) * scale).astype(bf16).astype(f32)
        p = jnp.exp2(s * scale - top)
        tops.append(top)
        totals.append(jnp.sum(p, axis=1, keepdims=True))
        outs.append(jnp.dot(p.astype(bf16), vbuf[b], preferred_element_type=f32))

    lane = lax.broadcasted_iota(jnp.int32, (rows, head_size), 1)

    def pack(top, total, o):
        o = o * (1.0 / total)
        high = total.astype(bf16).astype(f32)
        stats = jnp.where(lane == 0, top, jnp.where(lane == 1, high, total - high))
        o = o.reshape(STEPS, heads, head_size)
        stats = stats.reshape(STEPS, heads, head_size)
        return jnp.concatenate([o, stats], axis=1).astype(bf16)

    both_top = jnp.maximum(tops[0], tops[1])
    w0 = jnp.exp2(tops[0] - both_top)
    w1 = jnp.exp2(tops[1] - both_top)
    both = pack(both_top, w0 * totals[0] + w1 * totals[1], w0 * outs[0] + w1 * outs[1])
    same = request[0] == request[1]
    first = jnp.where(same, both, pack(tops[0], totals[0], outs[0]))
    second = jnp.where(same, both, pack(tops[1], totals[1], outs[1]))
    row = lax.broadcasted_iota(jnp.int32, (STEPS, 2 * heads, head_size), 1)
    lanes = lax.broadcasted_iota(jnp.int32, (STEPS, 2 * heads, head_size), 2)
    empty = jnp.where((row >= heads) & (lanes == 0), EMPTY, 0.0).astype(bf16)
    for r in range(requests):
        msg[r * STEPS : (r + 1) * STEPS] = jnp.where(
            request[0] == r, first, jnp.where(request[1] == r, second, empty)
        )
    def send_m(peer):
        pltpu.make_async_remote_copy(
            src_ref=msg.at[peer],
            dst_ref=got.at[me],
            send_sem=m_send,
            recv_sem=m_recv,
            device_id={"inst": peer},
            device_id_type=MESH,
        ).start()

    pl.when(me != 1)(lambda: send_m(1))
    for peer in plane:
        pl.when(peer != 1)(functools.partial(send_m, peer))
    got[me] = msg[me]
    w_copy.wait()
    m_others = got.at[pl.ds(0, n_inst - 1)]
    pltpu.make_async_copy(m_others, m_others, m_recv).wait()

    tile = got[...].astype(f32)
    o = tile[:, :heads]
    top = tile[:, heads:, 0:1]
    total = tile[:, heads:, 1:2] + tile[:, heads:, 2:3]
    best = jnp.max(top, axis=0, keepdims=True)
    weight = jnp.exp2(top - best) * total
    att = jnp.sum(weight * o, axis=0) / jnp.sum(weight, axis=0)
    att = jnp.concatenate([att[h : h + 1] for h in range(heads)], axis=1).astype(bf16)

    def project(peer):
        cols = pl.ds(pl.multiple_of(peer * out_cols, out_cols), out_cols)
        part[peer] = jnp.dot(att, wbuf[:, cols], preferred_element_type=f32)

    def send_p(peer):
        pltpu.make_async_remote_copy(
            src_ref=part.at[peer],
            dst_ref=parts.at[my_tp],
            send_sem=p_send,
            recv_sem=p_recv,
            device_id={"tp": peer},
            device_id_type=MESH,
        ).start()

    for peer in z_ring:
        project(peer)
        send_p(peer)
    project(my_tp)
    parts[my_tp] = part[my_tp]
    pltpu.make_async_copy(q_others, q_others, q_send).wait()
    pltpu.make_async_copy(m_others, m_others, m_send).wait()
    p_others = parts.at[pl.ds(0, n_tp - 1)]
    pltpu.make_async_copy(p_others, p_others, p_send).wait()
    pltpu.make_async_copy(p_others, p_others, p_recv).wait()
    out_ref[...] = jnp.sum(parts[...], axis=0).astype(out_ref.dtype)


def solution(mesh):
    n_inst, n_tp = mesh.shape["inst"], mesh.shape["tp"]

    def body(queries, cache_keys, cache_values, block_request, block_fill, out_weight):
        blocks, _, block_len, head_size = cache_keys.shape
        width, dout = out_weight.shape
        heads = width // head_size
        cols = dout // n_tp
        any_spec = pl.BlockSpec(memory_space=pl.ANY)
        dma = pltpu.SemaphoreType.DMA
        bf16, f32 = jnp.bfloat16, jnp.float32
        operands = [
            pltpu.with_memory_space_constraint(a, pltpu.HBM)
            for a in (
                block_request,
                block_fill,
                queries,
                cache_keys,
                cache_values,
                out_weight,
            )
        ]
        return pl.pallas_call(
            lambda *refs: kernel(n_tp, *refs),
            out_shape=jax.ShapeDtypeStruct((1, cols), bf16),
            in_specs=[any_spec] * 6,
            out_specs=pl.BlockSpec(memory_space=pltpu.VMEM),
            scratch_shapes=[
                pltpu.SMEM(block_request.shape, jnp.int32),
                pltpu.SMEM(block_fill.shape, jnp.int32),
                pltpu.VMEM(queries.shape, bf16),
                pltpu.VMEM((blocks, block_len, head_size), bf16),
                pltpu.VMEM((blocks, head_size, block_len), bf16),
                pltpu.VMEM((blocks, block_len, head_size), bf16),
                pltpu.VMEM((width, dout), bf16),
                pltpu.VMEM((n_inst, heads, head_size), bf16),
                pltpu.VMEM((n_inst, 2 * heads, head_size), bf16),
                pltpu.VMEM((n_inst, 2 * heads, head_size), bf16),
                pltpu.VMEM((n_tp, 1, cols), f32),
                pltpu.VMEM((n_tp, 1, cols), f32),
                dma((6,)),
                dma,
                dma,
                dma,
                dma,
                dma,
                dma,
            ],
            compiler_params=pltpu.CompilerParams(
                collective_id=0, has_side_effects=True, vmem_limit_bytes=40 * 1024 * 1024
            ),
            name="paged_decode",
        )(*operands)

    in_specs = (
        P("inst", "tp"),
        P("inst", "tp", None, None),
        P("inst", "tp", None, None),
        P(),
        P(),
        P("tp", None),
    )
    return jax.shard_map(
        body, mesh=mesh, in_specs=in_specs, out_specs=P("inst", "tp"), check_vma=False
    )
```

```python
import math

import jax
import jax.numpy as jnp
from jax import lax
from jax.experimental import pallas as pl
from jax.experimental.pallas import tpu as pltpu
from jax.sharding import PartitionSpec as P

MESH = pl.DeviceIdType.MESH
EMPTY = -1e30
STEPS = 4
SIDE = 4


def ring(d, n):
    return min(d, n - d)


CHIPS = sorted(
    [(x, y) for x in range(SIDE) for y in range(SIDE)][1:],
    key=lambda d: -(ring(d[0], SIDE) + ring(d[1], SIDE)),
)


def kernel(
    n_tp,
    req_hbm,
    fill_hbm,
    q_hbm,
    k_hbm,
    v_hbm,
    w_hbm,
    out_ref,
    req_ref,
    fill_ref,
    q_in,
    kbuf,
    kt,
    vbuf,
    wbuf,
    q_all,
    msg,
    got,
    part,
    parts,
    local_sem,
    pair_send,
    pair_recv,
    q_send,
    q_recv,
    m_send,
    m_recv,
    p_send,
    p_recv,
):
    me = lax.axis_index("inst")
    my_tp = lax.axis_index("tp")
    blocks, block_len, head_size = kbuf.shape
    n_inst, heads, _ = q_all.shape
    rows = STEPS * heads
    requests = n_inst // STEPS
    out_cols = part.shape[2]
    scale = head_size**-0.5 * math.log2(math.e)
    f32, bf16 = jnp.float32, jnp.bfloat16

    my_x, my_y, my_core = me // (2 * SIDE), (me // 2) % SIDE, me % 2
    chips = [((my_x + x) % SIDE) * SIDE + (my_y + y) % SIDE for x, y in CHIPS]
    sibling = me + 1 - 2 * my_core
    plane = [2 * chip + core for chip in chips for core in range(2)] + [sibling]
    z_ring = [
        (my_tp + d) % n_tp for d in sorted(range(1, n_tp), key=lambda d: -ring(d, n_tp))
    ]

    barrier = pltpu.get_barrier_semaphore()
    my_lead = me + 1 - my_core
    for chip in chips:
        pl.semaphore_signal(
            barrier, inc=1, device_id={"inst": 2 * chip + 1}, device_id_type=MESH
        )
    pl.semaphore_signal(barrier, inc=1, device_id={"inst": sibling}, device_id_type=MESH)
    for peer in z_ring:
        pl.semaphore_signal(
            barrier, inc=1, device_id={"inst": my_lead, "tp": peer}, device_id_type=MESH
        )

    q_copy = pltpu.make_async_copy(q_hbm, q_in, local_sem.at[0])
    req_copy = pltpu.make_async_copy(req_hbm, req_ref, local_sem.at[1])
    fill_copy = pltpu.make_async_copy(fill_hbm, fill_ref, local_sem.at[2])
    k_copy = pltpu.make_async_copy(k_hbm.at[:, 0], kbuf, local_sem.at[3])
    v_copy = pltpu.make_async_copy(v_hbm.at[:, 0], vbuf, local_sem.at[4])
    w_copy = pltpu.make_async_copy(w_hbm, wbuf, local_sem.at[5])
    for c in [q_copy, k_copy, req_copy, fill_copy, v_copy]:
        c.start()
    q_copy.wait()
    own_q = q_in[...].astype(f32)
    q_all[me] = jnp.concatenate(
        [own_q[:, h * head_size : (h + 1) * head_size] for h in range(heads)], axis=0
    ).astype(bf16)
    pair = pltpu.make_async_remote_copy(
        src_ref=q_all.at[me],
        dst_ref=q_all.at[me],
        send_sem=pair_send,
        recv_sem=pair_recv,
        device_id={"inst": sibling},
        device_id_type=MESH,
    )
    q_others = q_all.at[pl.ds(0, n_inst - 2)]

    @pl.when(my_core == 0)
    def _():
        pl.semaphore_wait(barrier, 1)
        pair.start()

    @pl.when(my_core == 1)
    def _():
        pl.semaphore_wait(barrier, 2 * len(chips) + 2 * len(z_ring) + 1)
        pair.wait_recv()
        rows_here = q_all.at[pl.ds(me - 1, 2)]
        for peer in plane[:-1]:
            pltpu.make_async_remote_copy(
                src_ref=rows_here,
                dst_ref=rows_here,
                send_sem=q_send,
                recv_sem=q_recv,
                device_id={"inst": peer},
                device_id_type=MESH,
            ).start()
        pair.start()

    w_copy.start()

    k_copy.wait()
    for b in range(blocks):
        kt[b] = kbuf[b].T
    req_copy.wait()
    fill_copy.wait()
    v_copy.wait()
    request = [req_ref[me * blocks + b] for b in range(blocks)]
    fill = [fill_ref[me * blocks + b] for b in range(blocks)]

    @pl.when(my_core == 0)
    def _():
        pair.wait_recv()

    pltpu.make_async_copy(q_others, q_others, q_recv).wait()

    scores = []
    for b in range(blocks):
        q = q_all[pl.ds(request[b] * STEPS, STEPS)].reshape(rows, head_size)
        scores.append(jnp.dot(q, kt[b], preferred_element_type=f32))
    tops, totals, probs = [], [], []
    for b in range(blocks):
        slot = lax.broadcasted_iota(jnp.int32, (rows, block_len), 1)
        s = jnp.where(slot < fill[b], scores[b], EMPTY)
        top = (jnp.max(s, axis=1, keepdims=True) * scale).astype(bf16).astype(f32)
        p = jnp.exp2(s * scale - top)
        tops.append(top)
        totals.append(jnp.sum(p, axis=1, keepdims=True))
        probs.append(p.astype(bf16))

    same = request[0] == request[1]
    top = jnp.maximum(tops[0], tops[1])
    w0, w1 = [jnp.exp2(t - top) for t in tops]
    total = w0 * totals[0] + w1 * totals[1]
    w0, w1 = w0 / total, w1 / total
    i0, i1 = 1.0 / totals[0], 1.0 / totals[1]
    zero = jnp.zeros_like(i0)
    weights = [
        (jnp.where(same, w0, i0), jnp.where(same, w1, zero)),
        (jnp.where(same, w0, zero), jnp.where(same, w1, i1)),
    ]
    half = head_size // 2
    lane = lax.broadcasted_iota(jnp.int32, (rows, head_size), 1)
    stats = []
    for b in range(blocks):
        m = jnp.where(same, top, tops[b])
        n = jnp.where(same, total, totals[b])
        stats.append(jnp.where(lane < half, m, n))
    outs = [jnp.dot(probs[b], vbuf[b], preferred_element_type=f32) for b in range(blocks)]
    shape = (STEPS, heads, head_size)
    first, second = [
        jnp.concatenate(
            [(u * outs[0] + v * outs[1]).reshape(shape), stats[b].reshape(shape)], axis=1
        ).astype(bf16)
        for b, (u, v) in enumerate(weights)
    ]
    row = lax.broadcasted_iota(jnp.int32, (STEPS, 2 * heads, head_size), 1)
    lanes = lax.broadcasted_iota(jnp.int32, (STEPS, 2 * heads, head_size), 2)
    empty = jnp.where((row >= heads) & (lanes < half), EMPTY, 0.0).astype(bf16)
    for r in range(requests):
        msg[r * STEPS : (r + 1) * STEPS] = jnp.where(
            request[0] == r, first, jnp.where(request[1] == r, second, empty)
        )
    def send_m(peer):
        pltpu.make_async_remote_copy(
            src_ref=msg.at[peer],
            dst_ref=got.at[me],
            send_sem=m_send,
            recv_sem=m_recv,
            device_id={"inst": peer},
            device_id_type=MESH,
        ).start()

    send_m(jnp.where(me == 1, plane[0], 1))
    for peer in plane[1:]:
        send_m(jnp.where((peer == 1) & (me != 1), plane[0], peer))
    got[me] = msg[me]
    w_copy.wait()
    m_others = got.at[pl.ds(0, n_inst - 1)]
    pltpu.make_async_copy(m_others, m_others, m_recv).wait()

    tile = got[...].astype(f32)
    o, stat = tile[:, :heads], tile[:, heads:]
    other = pltpu.roll(stat, half, 2)
    low = lax.broadcasted_iota(jnp.int32, stat.shape, 2) < half
    top = jnp.where(low, stat, other)
    weight = jnp.exp2(top - jnp.max(top, axis=0)) * jnp.where(low, other, stat)
    att = jnp.sum(weight * o, axis=0) * (1.0 / jnp.sum(weight, axis=0))
    att = jnp.concatenate([att[h : h + 1] for h in range(heads)], axis=1).astype(bf16)

    def project(peer):
        cols = pl.ds(pl.multiple_of(peer * out_cols, out_cols), out_cols)
        part[peer] = jnp.dot(att, wbuf[:, cols], preferred_element_type=f32)

    def send_p(peer):
        pltpu.make_async_remote_copy(
            src_ref=part.at[peer],
            dst_ref=parts.at[my_tp],
            send_sem=p_send,
            recv_sem=p_recv,
            device_id={"tp": peer},
            device_id_type=MESH,
        ).start()

    for peer in z_ring:
        project(peer)
        send_p(peer)
    project(my_tp)
    parts[my_tp] = part[my_tp]
    pair.wait_send()

    @pl.when(my_core == 1)
    def _():
        for _ in range(2):
            pltpu.make_async_copy(q_others, q_others, q_send).wait()

    pltpu.make_async_copy(m_others, m_others, m_send).wait()
    p_others = parts.at[pl.ds(0, n_tp - 1)]
    pltpu.make_async_copy(p_others, p_others, p_send).wait()
    pltpu.make_async_copy(p_others, p_others, p_recv).wait()
    out_ref[...] = jnp.sum(parts[...], axis=0).astype(out_ref.dtype)


def solution(mesh):
    n_inst, n_tp = mesh.shape["inst"], mesh.shape["tp"]

    def body(queries, cache_keys, cache_values, block_request, block_fill, out_weight):
        blocks, _, block_len, head_size = cache_keys.shape
        width, dout = out_weight.shape
        heads = width // head_size
        cols = dout // n_tp
        any_spec = pl.BlockSpec(memory_space=pl.ANY)
        dma = pltpu.SemaphoreType.DMA
        bf16, f32 = jnp.bfloat16, jnp.float32
        operands = [
            pltpu.with_memory_space_constraint(a, pltpu.HBM)
            for a in (
                block_request,
                block_fill,
                queries,
                cache_keys,
                cache_values,
                out_weight,
            )
        ]
        return pl.pallas_call(
            lambda *refs: kernel(n_tp, *refs),
            out_shape=jax.ShapeDtypeStruct((1, cols), bf16),
            in_specs=[any_spec] * 6,
            out_specs=pl.BlockSpec(memory_space=pltpu.VMEM),
            scratch_shapes=[
                pltpu.SMEM(block_request.shape, jnp.int32),
                pltpu.SMEM(block_fill.shape, jnp.int32),
                pltpu.VMEM(queries.shape, bf16),
                pltpu.VMEM((blocks, block_len, head_size), bf16),
                pltpu.VMEM((blocks, head_size, block_len), bf16),
                pltpu.VMEM((blocks, block_len, head_size), bf16),
                pltpu.VMEM((width, dout), bf16),
                pltpu.VMEM((n_inst, heads, head_size), bf16),
                pltpu.VMEM((n_inst, 2 * heads, head_size), bf16),
                pltpu.VMEM((n_inst, 2 * heads, head_size), bf16),
                pltpu.VMEM((n_tp, 1, cols), f32),
                pltpu.VMEM((n_tp, 1, cols), f32),
                dma((6,)),
                dma,
                dma,
                dma,
                dma,
                dma,
                dma,
                dma,
                dma,
            ],
            compiler_params=pltpu.CompilerParams(
                collective_id=0, has_side_effects=True, vmem_limit_bytes=40 * 1024 * 1024
            ),
            name="paged_decode",
        )(*operands)

    in_specs = (
        P("inst", "tp"),
        P("inst", "tp", None, None),
        P("inst", "tp", None, None),
        P(),
        P(),
        P("tp", None),
    )
    return jax.shard_map(
        body, mesh=mesh, in_specs=in_specs, out_specs=P("inst", "tp"), check_vma=False
    )
```

```python
import math

import jax
import jax.numpy as jnp
from jax import lax
from jax.experimental import pallas as pl
from jax.experimental.pallas import tpu as pltpu
from jax.sharding import PartitionSpec as P

MESH = pl.DeviceIdType.MESH
EMPTY = -1e30
STEPS = 4
SIDE = 4


def ring(d, n):
    return min(d, n - d)


CHIPS = sorted(
    [(x, y) for x in range(SIDE) for y in range(SIDE)][1:],
    key=lambda d: -(ring(d[0], SIDE) + ring(d[1], SIDE)),
)


def kernel(
    n_tp,
    req_hbm,
    fill_hbm,
    q_hbm,
    k_hbm,
    v_hbm,
    w_hbm,
    out_ref,
    req_ref,
    fill_ref,
    q_in,
    kbuf,
    kt,
    vbuf,
    wbuf,
    q_all,
    msg,
    got,
    part,
    parts,
    local_sem,
    go,
    pair_send,
    pair_recv,
    q_send,
    q_recv,
    m_send,
    m_recv,
    p_send,
    p_recv,
):
    me = lax.axis_index("inst")
    my_tp = lax.axis_index("tp")
    blocks, block_len, head_size = kbuf.shape
    n_inst, heads, _ = q_all.shape
    rows = STEPS * heads
    requests = n_inst // STEPS
    out_cols = part.shape[2]
    scale = head_size**-0.5 * math.log2(math.e)
    f32, bf16 = jnp.float32, jnp.bfloat16

    my_x, my_y, my_core = me // (2 * SIDE), (me // 2) % SIDE, me % 2
    chips = [((my_x + x) % SIDE) * SIDE + (my_y + y) % SIDE for x, y in CHIPS]
    sibling = me + 1 - 2 * my_core
    plane = [2 * chip + core for chip in chips for core in range(2)] + [sibling]
    z_ring = [
        (my_tp + d) % n_tp for d in sorted(range(1, n_tp), key=lambda d: -ring(d, n_tp))
    ]

    barrier = pltpu.get_barrier_semaphore()
    my_lead = me + 1 - my_core
    for chip in chips:
        pl.semaphore_signal(
            barrier, inc=1, device_id={"inst": 2 * chip + 1}, device_id_type=MESH
        )
    pl.semaphore_signal(barrier, inc=1, device_id={"inst": sibling}, device_id_type=MESH)
    for peer in z_ring:
        pl.semaphore_signal(
            barrier, inc=1, device_id={"inst": my_lead, "tp": peer}, device_id_type=MESH
        )

    q_copy = pltpu.make_async_copy(q_hbm, q_in, local_sem.at[0])
    req_copy = pltpu.make_async_copy(req_hbm, req_ref, local_sem.at[1])
    fill_copy = pltpu.make_async_copy(fill_hbm, fill_ref, local_sem.at[2])
    k_copy = pltpu.make_async_copy(k_hbm.at[:, 0], kbuf, local_sem.at[3])
    v_copy = pltpu.make_async_copy(v_hbm.at[:, 0], vbuf, local_sem.at[4])
    w_copy = pltpu.make_async_copy(w_hbm, wbuf, local_sem.at[5])
    for c in [q_copy, k_copy, req_copy, fill_copy, v_copy]:
        c.start()
    q_copy.wait()
    own_q = q_in[...].astype(f32)
    q_all[me] = jnp.concatenate(
        [own_q[:, h * head_size : (h + 1) * head_size] for h in range(heads)], axis=0
    ).astype(bf16)
    pair = pltpu.make_async_remote_copy(
        src_ref=q_all.at[me],
        dst_ref=q_all.at[me],
        send_sem=pair_send,
        recv_sem=pair_recv,
        device_id={"inst": sibling},
        device_id_type=MESH,
    )
    q_others = q_all.at[pl.ds(0, n_inst - 2)]

    rows_here = q_all.at[pl.ds(my_lead - 1, 2)]

    def send_q(core):
        for chip in chips:
            pltpu.make_async_remote_copy(
                src_ref=rows_here,
                dst_ref=rows_here,
                send_sem=q_send,
                recv_sem=q_recv,
                device_id={"inst": 2 * chip + core},
                device_id_type=MESH,
            ).start()

    @pl.when(my_core == 0)
    def _():
        pl.semaphore_wait(barrier, 1)
        pair.start()
        pair.wait_recv()
        pl.semaphore_wait(go, 1)
        send_q(1)

    @pl.when(my_core == 1)
    def _():
        pair.wait_recv()
        pair.start()
        pl.semaphore_wait(barrier, 2 * len(chips) + 2 * len(z_ring) + 1)
        pl.semaphore_signal(go, inc=1, device_id={"inst": sibling}, device_id_type=MESH)
        send_q(0)

    w_copy.start()

    k_copy.wait()
    for b in range(blocks):
        kt[b] = kbuf[b].T
    req_copy.wait()
    fill_copy.wait()
    v_copy.wait()
    request = [req_ref[me * blocks + b] for b in range(blocks)]
    fill = [fill_ref[me * blocks + b] for b in range(blocks)]

    pltpu.make_async_copy(q_others, q_others, q_recv).wait()

    scores = []
    for b in range(blocks):
        q = q_all[pl.ds(request[b] * STEPS, STEPS)].reshape(rows, head_size)
        scores.append(jnp.dot(q, kt[b], preferred_element_type=f32))
    tops, totals, probs = [], [], []
    for b in range(blocks):
        slot = lax.broadcasted_iota(jnp.int32, (rows, block_len), 1)
        s = jnp.where(slot < fill[b], scores[b], EMPTY)
        top = (jnp.max(s, axis=1, keepdims=True) * scale).astype(bf16).astype(f32)
        p = jnp.exp2(s * scale - top)
        tops.append(top)
        totals.append(jnp.sum(p, axis=1, keepdims=True))
        probs.append(p.astype(bf16))

    same = request[0] == request[1]
    top = jnp.maximum(tops[0], tops[1])
    w0, w1 = [jnp.exp2(t - top) for t in tops]
    total = w0 * totals[0] + w1 * totals[1]
    w0, w1 = w0 / total, w1 / total
    i0, i1 = 1.0 / totals[0], 1.0 / totals[1]
    zero = jnp.zeros_like(i0)
    weights = [
        (jnp.where(same, w0, i0), jnp.where(same, w1, zero)),
        (jnp.where(same, w0, zero), jnp.where(same, w1, i1)),
    ]
    half = head_size // 2
    lane = lax.broadcasted_iota(jnp.int32, (rows, head_size), 1)
    stats = []
    for b in range(blocks):
        m = jnp.where(same, top, tops[b])
        n = jnp.where(same, total, totals[b])
        stats.append(jnp.where(lane < half, m, n))
    outs = [jnp.dot(probs[b], vbuf[b], preferred_element_type=f32) for b in range(blocks)]
    shape = (STEPS, heads, head_size)
    first, second = [
        jnp.concatenate(
            [(u * outs[0] + v * outs[1]).reshape(shape), stats[b].reshape(shape)], axis=1
        ).astype(bf16)
        for b, (u, v) in enumerate(weights)
    ]
    row = lax.broadcasted_iota(jnp.int32, (STEPS, 2 * heads, head_size), 1)
    lanes = lax.broadcasted_iota(jnp.int32, (STEPS, 2 * heads, head_size), 2)
    empty = jnp.where((row >= heads) & (lanes < half), EMPTY, 0.0).astype(bf16)
    for r in range(requests):
        msg[r * STEPS : (r + 1) * STEPS] = jnp.where(
            request[0] == r, first, jnp.where(request[1] == r, second, empty)
        )
    def send_m(peer):
        pltpu.make_async_remote_copy(
            src_ref=msg.at[peer],
            dst_ref=got.at[me],
            send_sem=m_send,
            recv_sem=m_recv,
            device_id={"inst": peer},
            device_id_type=MESH,
        ).start()

    send_m(jnp.where(me == 1, plane[0], 1))
    for peer in plane[1:]:
        send_m(jnp.where((peer == 1) & (me != 1), plane[0], peer))
    got[me] = msg[me]
    w_copy.wait()
    m_others = got.at[pl.ds(0, n_inst - 1)]
    pltpu.make_async_copy(m_others, m_others, m_recv).wait()

    tile = got[...].astype(f32)
    o, stat = tile[:, :heads], tile[:, heads:]
    other = pltpu.roll(stat, half, 2)
    low = lax.broadcasted_iota(jnp.int32, stat.shape, 2) < half
    top = jnp.where(low, stat, other)
    weight = jnp.exp2(top - jnp.max(top, axis=0)) * jnp.where(low, other, stat)
    att = jnp.sum(weight * o, axis=0) * (1.0 / jnp.sum(weight, axis=0))
    att = jnp.concatenate([att[h : h + 1] for h in range(heads)], axis=1).astype(bf16)

    def project(peer):
        cols = pl.ds(pl.multiple_of(peer * out_cols, out_cols), out_cols)
        part[peer] = jnp.dot(att, wbuf[:, cols], preferred_element_type=f32)

    def send_p(peer):
        pltpu.make_async_remote_copy(
            src_ref=part.at[peer],
            dst_ref=parts.at[my_tp],
            send_sem=p_send,
            recv_sem=p_recv,
            device_id={"tp": peer},
            device_id_type=MESH,
        ).start()

    for peer in z_ring:
        project(peer)
        send_p(peer)
    project(my_tp)
    parts[my_tp] = part[my_tp]
    pair.wait_send()

    pltpu.make_async_copy(q_others, q_others, q_send).wait()

    pltpu.make_async_copy(m_others, m_others, m_send).wait()
    p_others = parts.at[pl.ds(0, n_tp - 1)]
    pltpu.make_async_copy(p_others, p_others, p_send).wait()
    pltpu.make_async_copy(p_others, p_others, p_recv).wait()
    out_ref[...] = jnp.sum(parts[...], axis=0).astype(out_ref.dtype)


def solution(mesh):
    n_inst, n_tp = mesh.shape["inst"], mesh.shape["tp"]

    def body(queries, cache_keys, cache_values, block_request, block_fill, out_weight):
        blocks, _, block_len, head_size = cache_keys.shape
        width, dout = out_weight.shape
        heads = width // head_size
        cols = dout // n_tp
        any_spec = pl.BlockSpec(memory_space=pl.ANY)
        dma = pltpu.SemaphoreType.DMA
        bf16, f32 = jnp.bfloat16, jnp.float32
        operands = [
            pltpu.with_memory_space_constraint(a, pltpu.HBM)
            for a in (
                block_request,
                block_fill,
                queries,
                cache_keys,
                cache_values,
                out_weight,
            )
        ]
        return pl.pallas_call(
            lambda *refs: kernel(n_tp, *refs),
            out_shape=jax.ShapeDtypeStruct((1, cols), bf16),
            in_specs=[any_spec] * 6,
            out_specs=pl.BlockSpec(memory_space=pltpu.VMEM),
            scratch_shapes=[
                pltpu.SMEM(block_request.shape, jnp.int32),
                pltpu.SMEM(block_fill.shape, jnp.int32),
                pltpu.VMEM(queries.shape, bf16),
                pltpu.VMEM((blocks, block_len, head_size), bf16),
                pltpu.VMEM((blocks, head_size, block_len), bf16),
                pltpu.VMEM((blocks, block_len, head_size), bf16),
                pltpu.VMEM((width, dout), bf16),
                pltpu.VMEM((n_inst, heads, head_size), bf16),
                pltpu.VMEM((n_inst, 2 * heads, head_size), bf16),
                pltpu.VMEM((n_inst, 2 * heads, head_size), bf16),
                pltpu.VMEM((n_tp, 1, cols), f32),
                pltpu.VMEM((n_tp, 1, cols), f32),
                dma((6,)),
                pltpu.SemaphoreType.REGULAR,
                dma,
                dma,
                dma,
                dma,
                dma,
                dma,
                dma,
                dma,
            ],
            compiler_params=pltpu.CompilerParams(
                collective_id=0, has_side_effects=True, vmem_limit_bytes=40 * 1024 * 1024
            ),
            name="paged_decode",
        )(*operands)

    in_specs = (
        P("inst", "tp"),
        P("inst", "tp", None, None),
        P("inst", "tp", None, None),
        P(),
        P(),
        P("tp", None),
    )
    return jax.shard_map(
        body, mesh=mesh, in_specs=in_specs, out_specs=P("inst", "tp"), check_vma=False
    )
```

```python
import math

import jax
import jax.numpy as jnp
from jax import lax
from jax.experimental import pallas as pl
from jax.experimental.pallas import tpu as pltpu
from jax.sharding import PartitionSpec as P

MESH = pl.DeviceIdType.MESH
EMPTY = -1e30
STEPS = 4
SIDE = 4


def ring(d, n):
    return min(d, n - d)


CHIPS = sorted(
    [(x, y) for x in range(SIDE) for y in range(SIDE)][1:],
    key=lambda d: -(ring(d[0], SIDE) + ring(d[1], SIDE)),
)


def kernel(
    n_tp,
    req_hbm,
    fill_hbm,
    q_hbm,
    k_hbm,
    v_hbm,
    w_hbm,
    out_ref,
    req_ref,
    fill_ref,
    q_in,
    kbuf,
    kt,
    vbuf,
    wbuf,
    q_own,
    q_other,
    q_all,
    msg,
    got,
    part,
    parts,
    local_sem,
    go,
    pair_send,
    pair_recv,
    q_send,
    q_recv,
    m_send,
    m_recv,
    p_send,
    p_recv,
):
    me = lax.axis_index("inst")
    my_tp = lax.axis_index("tp")
    blocks, block_len, head_size = kbuf.shape
    n_inst, heads = msg.shape[0], q_own.shape[0]
    rows = STEPS * heads
    requests = n_inst // STEPS
    out_cols = part.shape[2]
    scale = head_size**-0.5 * math.log2(math.e)
    f32, bf16 = jnp.float32, jnp.bfloat16

    my_x, my_y, my_core = me // (2 * SIDE), (me // 2) % SIDE, me % 2
    chips = [((my_x + x) % SIDE) * SIDE + (my_y + y) % SIDE for x, y in CHIPS]
    sibling = me + 1 - 2 * my_core
    plane = [2 * chip + core for chip in chips for core in range(2)] + [sibling]
    z_ring = [
        (my_tp + d) % n_tp for d in sorted(range(1, n_tp), key=lambda d: -ring(d, n_tp))
    ]

    barrier = pltpu.get_barrier_semaphore()
    my_lead = me + 1 - my_core
    for chip in chips:
        pl.semaphore_signal(
            barrier, inc=1, device_id={"inst": 2 * chip + 1}, device_id_type=MESH
        )
    pl.semaphore_signal(barrier, inc=1, device_id={"inst": sibling}, device_id_type=MESH)
    for peer in z_ring:
        pl.semaphore_signal(
            barrier, inc=1, device_id={"inst": my_lead, "tp": peer}, device_id_type=MESH
        )

    q_copy = pltpu.make_async_copy(q_hbm, q_in, local_sem.at[0])
    req_copy = pltpu.make_async_copy(req_hbm, req_ref, local_sem.at[1])
    fill_copy = pltpu.make_async_copy(fill_hbm, fill_ref, local_sem.at[2])
    k_copy = pltpu.make_async_copy(k_hbm.at[:, 0], kbuf, local_sem.at[3])
    v_copy = pltpu.make_async_copy(v_hbm.at[:, 0], vbuf, local_sem.at[4])
    w_copy = pltpu.make_async_copy(w_hbm, wbuf, local_sem.at[5])
    for c in [q_copy, k_copy, req_copy, fill_copy, v_copy]:
        c.start()
    q_copy.wait()
    own_q = q_in[...].astype(f32)
    q_own[...] = jnp.concatenate(
        [own_q[:, h * head_size : (h + 1) * head_size] for h in range(heads)], axis=0
    )

    pair = pltpu.make_async_remote_copy(
        src_ref=q_own,
        dst_ref=q_other,
        send_sem=pair_send,
        recv_sem=pair_recv,
        device_id={"inst": sibling},
        device_id_type=MESH,
    )
    q_others = q_all.at[pl.ds(0, len(chips))]

    rows_here = q_all.at[me // 2]

    def join():
        own, other = q_own[...], q_other[...]
        low, high = jnp.where(my_core == 0, own, other), jnp.where(my_core == 0, other, own)
        q_all[me // 2] = jnp.concatenate([low, high], axis=0).astype(bf16)

    def send_q(core):
        for chip in chips:
            pltpu.make_async_remote_copy(
                src_ref=rows_here,
                dst_ref=rows_here,
                send_sem=q_send,
                recv_sem=q_recv,
                device_id={"inst": 2 * chip + core},
                device_id_type=MESH,
            ).start()

    @pl.when(my_core == 0)
    def _():
        pl.semaphore_wait(barrier, 1)
        pair.start()
        pair.wait_recv()
        join()
        pl.semaphore_wait(go, 1)
        send_q(1)

    @pl.when(my_core == 1)
    def _():
        pair.wait_recv()
        pair.start()
        join()
        pl.semaphore_wait(barrier, 2 * len(chips) + 2 * len(z_ring) + 1)
        pl.semaphore_signal(go, inc=1, device_id={"inst": sibling}, device_id_type=MESH)
        send_q(0)

    w_copy.start()

    k_copy.wait()
    for b in range(blocks):
        kt[b] = kbuf[b].T
    req_copy.wait()
    fill_copy.wait()
    v_copy.wait()
    request = [req_ref[me * blocks + b] for b in range(blocks)]
    fill = [fill_ref[me * blocks + b] for b in range(blocks)]

    pltpu.make_async_copy(q_others, q_others, q_recv).wait()

    scores = []
    for b in range(blocks):
        q = q_all[pl.ds(request[b] * (STEPS // 2), STEPS // 2)].reshape(rows, head_size)
        scores.append(jnp.dot(q, kt[b], preferred_element_type=f32))
    tops, totals, probs = [], [], []
    for b in range(blocks):
        slot = lax.broadcasted_iota(jnp.int32, (rows, block_len), 1)
        s = jnp.where(slot < fill[b], scores[b], EMPTY)
        top = (jnp.max(s, axis=1, keepdims=True) * scale).astype(bf16).astype(f32)
        p = jnp.exp2(s * scale - top)
        tops.append(top)
        totals.append(jnp.sum(p, axis=1, keepdims=True))
        probs.append(p.astype(bf16))

    same = request[0] == request[1]
    top = jnp.maximum(tops[0], tops[1])
    w0, w1 = [jnp.exp2(t - top) for t in tops]
    total = w0 * totals[0] + w1 * totals[1]
    w0, w1 = w0 / total, w1 / total
    i0, i1 = 1.0 / totals[0], 1.0 / totals[1]
    zero = jnp.zeros_like(i0)
    weights = [
        (jnp.where(same, w0, i0), jnp.where(same, w1, zero)),
        (jnp.where(same, w0, zero), jnp.where(same, w1, i1)),
    ]
    half = head_size // 2
    lane = lax.broadcasted_iota(jnp.int32, (rows, head_size), 1)
    stats = []
    for b in range(blocks):
        m = jnp.where(same, top, tops[b])
        n = jnp.where(same, total, totals[b])
        stats.append(jnp.where(lane < half, m, n))
    outs = [jnp.dot(probs[b], vbuf[b], preferred_element_type=f32) for b in range(blocks)]
    shape = (STEPS, heads, head_size)
    first, second = [
        jnp.concatenate(
            [(u * outs[0] + v * outs[1]).reshape(shape), stats[b].reshape(shape)], axis=1
        ).astype(bf16)
        for b, (u, v) in enumerate(weights)
    ]
    row = lax.broadcasted_iota(jnp.int32, (STEPS, 2 * heads, head_size), 1)
    lanes = lax.broadcasted_iota(jnp.int32, (STEPS, 2 * heads, head_size), 2)
    empty = jnp.where((row >= heads) & (lanes < half), EMPTY, 0.0).astype(bf16)
    for r in range(requests):
        msg[r * STEPS : (r + 1) * STEPS] = jnp.where(
            request[0] == r, first, jnp.where(request[1] == r, second, empty)
        )
    def send_m(peer):
        pltpu.make_async_remote_copy(
            src_ref=msg.at[peer],
            dst_ref=got.at[me],
            send_sem=m_send,
            recv_sem=m_recv,
            device_id={"inst": peer},
            device_id_type=MESH,
        ).start()

    send_m(jnp.where(me == 1, plane[0], 1))
    for peer in plane[1:]:
        send_m(jnp.where((peer == 1) & (me != 1), plane[0], peer))
    got[me] = msg[me]
    w_copy.wait()
    m_others = got.at[pl.ds(0, n_inst - 1)]
    pltpu.make_async_copy(m_others, m_others, m_recv).wait()

    tile = got[...].astype(f32)
    o, stat = tile[:, :heads], tile[:, heads:]
    other = pltpu.roll(stat, half, 2)
    low = lax.broadcasted_iota(jnp.int32, stat.shape, 2) < half
    top = jnp.where(low, stat, other)
    weight = jnp.exp2(top - jnp.max(top, axis=0)) * jnp.where(low, other, stat)
    att = jnp.sum(weight * o, axis=0) * (1.0 / jnp.sum(weight, axis=0))
    att = jnp.concatenate([att[h : h + 1] for h in range(heads)], axis=1).astype(bf16)

    def project(peer):
        cols = pl.ds(pl.multiple_of(peer * out_cols, out_cols), out_cols)
        part[peer] = jnp.dot(att, wbuf[:, cols], preferred_element_type=f32)

    def send_p(peer):
        pltpu.make_async_remote_copy(
            src_ref=part.at[peer],
            dst_ref=parts.at[my_tp],
            send_sem=p_send,
            recv_sem=p_recv,
            device_id={"tp": peer},
            device_id_type=MESH,
        ).start()

    for peer in z_ring:
        project(peer)
        send_p(peer)
    project(my_tp)
    parts[my_tp] = part[my_tp]
    pair.wait_send()

    pltpu.make_async_copy(q_others, q_others, q_send).wait()

    pltpu.make_async_copy(m_others, m_others, m_send).wait()
    p_others = parts.at[pl.ds(0, n_tp - 1)]
    pltpu.make_async_copy(p_others, p_others, p_send).wait()
    pltpu.make_async_copy(p_others, p_others, p_recv).wait()
    out_ref[...] = jnp.sum(parts[...], axis=0).astype(out_ref.dtype)


def solution(mesh):
    n_inst, n_tp = mesh.shape["inst"], mesh.shape["tp"]

    def body(queries, cache_keys, cache_values, block_request, block_fill, out_weight):
        blocks, _, block_len, head_size = cache_keys.shape
        width, dout = out_weight.shape
        heads = width // head_size
        cols = dout // n_tp
        any_spec = pl.BlockSpec(memory_space=pl.ANY)
        dma = pltpu.SemaphoreType.DMA
        bf16, f32 = jnp.bfloat16, jnp.float32
        operands = [
            pltpu.with_memory_space_constraint(a, pltpu.HBM)
            for a in (
                block_request,
                block_fill,
                queries,
                cache_keys,
                cache_values,
                out_weight,
            )
        ]
        return pl.pallas_call(
            lambda *refs: kernel(n_tp, *refs),
            out_shape=jax.ShapeDtypeStruct((1, cols), bf16),
            in_specs=[any_spec] * 6,
            out_specs=pl.BlockSpec(memory_space=pltpu.VMEM),
            scratch_shapes=[
                pltpu.SMEM(block_request.shape, jnp.int32),
                pltpu.SMEM(block_fill.shape, jnp.int32),
                pltpu.VMEM(queries.shape, bf16),
                pltpu.VMEM((blocks, block_len, head_size), bf16),
                pltpu.VMEM((blocks, head_size, block_len), bf16),
                pltpu.VMEM((blocks, block_len, head_size), bf16),
                pltpu.VMEM((width, dout), bf16),
                pltpu.VMEM((heads, head_size), f32),
                pltpu.VMEM((heads, head_size), f32),
                pltpu.VMEM((n_inst // 2, 2 * heads, head_size), bf16),
                pltpu.VMEM((n_inst, 2 * heads, head_size), bf16),
                pltpu.VMEM((n_inst, 2 * heads, head_size), bf16),
                pltpu.VMEM((n_tp, 1, cols), f32),
                pltpu.VMEM((n_tp, 1, cols), f32),
                dma((6,)),
                pltpu.SemaphoreType.REGULAR,
                dma,
                dma,
                dma,
                dma,
                dma,
                dma,
                dma,
                dma,
            ],
            compiler_params=pltpu.CompilerParams(
                collective_id=0, has_side_effects=True, vmem_limit_bytes=40 * 1024 * 1024
            ),
            name="paged_decode",
        )(*operands)

    in_specs = (
        P("inst", "tp"),
        P("inst", "tp", None, None),
        P("inst", "tp", None, None),
        P(),
        P(),
        P("tp", None),
    )
    return jax.shard_map(
        body, mesh=mesh, in_specs=in_specs, out_specs=P("inst", "tp"), check_vma=False
    )
```

```python
import functools
import math

import jax
import jax.numpy as jnp
from jax import lax
from jax.experimental import pallas as pl
from jax.experimental.pallas import tpu as pltpu
from jax.sharding import PartitionSpec as P

MESH = pl.DeviceIdType.MESH
EMPTY = -1e30
STEPS = 4
SIDE = 4


def ring(d, n):
    return min(d, n - d)


CHIPS = sorted(
    [(x, y) for x in range(SIDE) for y in range(SIDE)][1:],
    key=lambda d: -(ring(d[0], SIDE) + ring(d[1], SIDE)),
)


def kernel(
    n_tp,
    req_hbm,
    fill_hbm,
    q_hbm,
    k_hbm,
    v_hbm,
    w_hbm,
    out_ref,
    req_ref,
    fill_ref,
    q_in,
    kbuf,
    kt,
    vbuf,
    wbuf,
    q_own,
    q_other,
    q_all,
    msg,
    got,
    part,
    parts,
    local_sem,
    go,
    pair_send,
    pair_recv,
    q_send,
    q_recv,
    f_send,
    m_send,
    m_recv,
    p_send,
    p_recv,
):
    me = lax.axis_index("inst")
    my_tp = lax.axis_index("tp")
    blocks, block_len, head_size = kbuf.shape
    n_inst, heads = msg.shape[0], q_own.shape[0]
    rows = STEPS * heads
    requests = n_inst // STEPS
    out_cols = part.shape[2]
    scale = head_size**-0.5 * math.log2(math.e)
    f32, bf16 = jnp.float32, jnp.bfloat16

    my_x, my_y, my_core = me // (2 * SIDE), (me // 2) % SIDE, me % 2
    chips = [((my_x + x) % SIDE) * SIDE + (my_y + y) % SIDE for x, y in CHIPS]
    sibling = me + 1 - 2 * my_core
    plane = [2 * chip + core for chip in chips for core in range(2)] + [sibling]
    z_ring = [
        (my_tp + d) % n_tp for d in sorted(range(1, n_tp), key=lambda d: -ring(d, n_tp))
    ]

    barrier = pltpu.get_barrier_semaphore()
    my_lead = me + 1 - my_core
    for chip in chips:
        pl.semaphore_signal(
            barrier, inc=1, device_id={"inst": 2 * chip + 1}, device_id_type=MESH
        )
    pl.semaphore_signal(barrier, inc=1, device_id={"inst": sibling}, device_id_type=MESH)
    for peer in z_ring:
        pl.semaphore_signal(
            barrier, inc=1, device_id={"inst": my_lead, "tp": peer}, device_id_type=MESH
        )

    q_copy = pltpu.make_async_copy(q_hbm, q_in, local_sem.at[0])
    req_copy = pltpu.make_async_copy(req_hbm, req_ref, local_sem.at[1])
    fill_copy = pltpu.make_async_copy(fill_hbm, fill_ref, local_sem.at[2])
    k_copy = pltpu.make_async_copy(k_hbm.at[:, 0], kbuf, local_sem.at[3])
    v_copy = pltpu.make_async_copy(v_hbm.at[:, 0], vbuf, local_sem.at[4])
    w_copy = pltpu.make_async_copy(w_hbm, wbuf, local_sem.at[5])
    for c in [q_copy, k_copy, req_copy, fill_copy, v_copy]:
        c.start()
    q_copy.wait()
    own_q = q_in[...].astype(f32)
    q_own[...] = jnp.concatenate(
        [own_q[:, h * head_size : (h + 1) * head_size] for h in range(heads)], axis=0
    )

    pair = pltpu.make_async_remote_copy(
        src_ref=q_own,
        dst_ref=q_other,
        send_sem=pair_send,
        recv_sem=pair_recv,
        device_id={"inst": sibling},
        device_id_type=MESH,
    )
    q_others = q_all.at[pl.ds(0, len(chips))]

    rows_here = q_all.at[me // 2]

    def join():
        own, other = q_own[...], q_other[...]
        low, high = jnp.where(my_core == 0, own, other), jnp.where(my_core == 0, other, own)
        q_all[me // 2] = jnp.concatenate([low, high], axis=0).astype(bf16)

    def send_q(core):
        for chip in chips:
            pltpu.make_async_remote_copy(
                src_ref=rows_here,
                dst_ref=rows_here,
                send_sem=q_send,
                recv_sem=q_recv,
                device_id={"inst": 2 * chip + core},
                device_id_type=MESH,
            ).start()

    @pl.when(my_core == 0)
    def _():
        pl.semaphore_wait(barrier, 1)
        pair.start()
        pair.wait_recv()
        join()
        pl.semaphore_wait(go, 1)
        send_q(1)

    @pl.when(my_core == 1)
    def _():
        pair.wait_recv()
        pair.start()
        join()
        pl.semaphore_wait(barrier, 2 * len(chips) + 2 * len(z_ring) + 1)
        pl.semaphore_signal(go, inc=1, device_id={"inst": sibling}, device_id_type=MESH)
        send_q(0)

    w_copy.start()

    k_copy.wait()
    for b in range(blocks):
        kt[b] = kbuf[b].T
    req_copy.wait()
    fill_copy.wait()
    v_copy.wait()
    request = [req_ref[me * blocks + b] for b in range(blocks)]
    fill = [fill_ref[me * blocks + b] for b in range(blocks)]

    pltpu.make_async_copy(q_others, q_others, q_recv).wait()

    scores = []
    for b in range(blocks):
        q = q_all[pl.ds(request[b] * (STEPS // 2), STEPS // 2)].reshape(rows, head_size)
        scores.append(jnp.dot(q, kt[b], preferred_element_type=f32))
    tops, totals, probs = [], [], []
    for b in range(blocks):
        slot = lax.broadcasted_iota(jnp.int32, (rows, block_len), 1)
        s = jnp.where(slot < fill[b], scores[b], EMPTY)
        top = (jnp.max(s, axis=1, keepdims=True) * scale).astype(bf16).astype(f32)
        p = jnp.exp2(s * scale - top)
        tops.append(top)
        totals.append(jnp.sum(p, axis=1, keepdims=True))
        probs.append(p.astype(bf16))

    same = request[0] == request[1]
    top = jnp.maximum(tops[0], tops[1])
    w0, w1 = [jnp.exp2(t - top) for t in tops]
    total = w0 * totals[0] + w1 * totals[1]
    w0, w1 = w0 / total, w1 / total
    i0, i1 = 1.0 / totals[0], 1.0 / totals[1]
    zero = jnp.zeros_like(i0)
    weights = [
        (jnp.where(same, w0, i0), jnp.where(same, w1, zero)),
        (jnp.where(same, w0, zero), jnp.where(same, w1, i1)),
    ]
    half = head_size // 2
    lane = lax.broadcasted_iota(jnp.int32, (rows, head_size), 1)
    stats = []
    for b in range(blocks):
        m = jnp.where(same, top, tops[b])
        n = jnp.where(same, total, totals[b])
        stats.append(jnp.where(lane < half, m, n))
    outs = [jnp.dot(probs[b], vbuf[b], preferred_element_type=f32) for b in range(blocks)]
    shape = (STEPS, heads, head_size)
    first, second = [
        jnp.concatenate(
            [(u * outs[0] + v * outs[1]).reshape(shape), stats[b].reshape(shape)], axis=1
        ).astype(bf16)
        for b, (u, v) in enumerate(weights)
    ]
    row = lax.broadcasted_iota(jnp.int32, (STEPS, 2 * heads, head_size), 1)
    lanes = lax.broadcasted_iota(jnp.int32, (STEPS, 2 * heads, head_size), 2)
    empty = jnp.where((row >= heads) & (lanes < half), EMPTY, 0.0).astype(bf16)
    def send_m(peer):
        pltpu.make_async_remote_copy(
            src_ref=msg.at[peer],
            dst_ref=got.at[me],
            send_sem=m_send,
            recv_sem=m_recv,
            device_id={"inst": peer},
            device_id_type=MESH,
        ).start()

    def fill_m(r, begin, end):
        msg[r * STEPS + begin : r * STEPS + end] = jnp.where(
            request[0] == r,
            first[begin:end],
            jnp.where(request[1] == r, second[begin:end], empty[begin:end]),
        )

    fill_m(0, 1, 2)
    first_m = pltpu.make_async_remote_copy(
        src_ref=msg.at[1],
        dst_ref=got.at[me],
        send_sem=f_send,
        recv_sem=m_recv,
        device_id={"inst": 1},
        device_id_type=MESH,
    )
    pl.when(me != 1)(first_m.start)
    fill_m(0, 0, 1)
    fill_m(0, 2, STEPS)
    for r in range(1, requests):
        fill_m(r, 0, STEPS)
    for chip in chips:
        send_m(2 * chip)
    pl.when(my_core == 1)(lambda: send_m(sibling))
    pl.when(me != 1)(first_m.wait_send)
    for chip in chips:
        pl.when(chip != 0)(functools.partial(send_m, 2 * chip + 1))
    pl.when((my_core == 0) & (me != 0))(lambda: send_m(sibling))
    got[me] = msg[me]
    w_copy.wait()
    m_others = got.at[pl.ds(0, n_inst - 1)]
    pltpu.make_async_copy(m_others, m_others, m_recv).wait()

    tile = got[...].astype(f32)
    o, stat = tile[:, :heads], tile[:, heads:]
    other = pltpu.roll(stat, half, 2)
    low = lax.broadcasted_iota(jnp.int32, stat.shape, 2) < half
    top = jnp.where(low, stat, other)
    weight = jnp.exp2(top - jnp.max(top, axis=0)) * jnp.where(low, other, stat)
    att = jnp.sum(weight * o, axis=0) * (1.0 / jnp.sum(weight, axis=0))
    att = jnp.concatenate([att[h : h + 1] for h in range(heads)], axis=1).astype(bf16)

    def project(peer):
        cols = pl.ds(pl.multiple_of(peer * out_cols, out_cols), out_cols)
        part[peer] = jnp.dot(att, wbuf[:, cols], preferred_element_type=f32)

    def send_p(peer):
        pltpu.make_async_remote_copy(
            src_ref=part.at[peer],
            dst_ref=parts.at[my_tp],
            send_sem=p_send,
            recv_sem=p_recv,
            device_id={"tp": peer},
            device_id_type=MESH,
        ).start()

    for peer in z_ring:
        project(peer)
        send_p(peer)
    project(my_tp)
    parts[my_tp] = part[my_tp]
    pair.wait_send()

    pltpu.make_async_copy(q_others, q_others, q_send).wait()

    m_sent = msg.at[pl.ds(0, n_inst - 2)]
    pltpu.make_async_copy(m_sent, m_sent, m_send).wait()

    @pl.when(me == 1)
    def _():
        pltpu.make_async_copy(msg.at[0], msg.at[0], m_send).wait()

    p_others = parts.at[pl.ds(0, n_tp - 1)]
    pltpu.make_async_copy(p_others, p_others, p_send).wait()
    pltpu.make_async_copy(p_others, p_others, p_recv).wait()
    out_ref[...] = jnp.sum(parts[...], axis=0).astype(out_ref.dtype)


def solution(mesh):
    n_inst, n_tp = mesh.shape["inst"], mesh.shape["tp"]

    def body(queries, cache_keys, cache_values, block_request, block_fill, out_weight):
        blocks, _, block_len, head_size = cache_keys.shape
        width, dout = out_weight.shape
        heads = width // head_size
        cols = dout // n_tp
        any_spec = pl.BlockSpec(memory_space=pl.ANY)
        dma = pltpu.SemaphoreType.DMA
        bf16, f32 = jnp.bfloat16, jnp.float32
        operands = [
            pltpu.with_memory_space_constraint(a, pltpu.HBM)
            for a in (
                block_request,
                block_fill,
                queries,
                cache_keys,
                cache_values,
                out_weight,
            )
        ]
        return pl.pallas_call(
            lambda *refs: kernel(n_tp, *refs),
            out_shape=jax.ShapeDtypeStruct((1, cols), bf16),
            in_specs=[any_spec] * 6,
            out_specs=pl.BlockSpec(memory_space=pltpu.VMEM),
            scratch_shapes=[
                pltpu.SMEM(block_request.shape, jnp.int32),
                pltpu.SMEM(block_fill.shape, jnp.int32),
                pltpu.VMEM(queries.shape, bf16),
                pltpu.VMEM((blocks, block_len, head_size), bf16),
                pltpu.VMEM((blocks, head_size, block_len), bf16),
                pltpu.VMEM((blocks, block_len, head_size), bf16),
                pltpu.VMEM((width, dout), bf16),
                pltpu.VMEM((heads, head_size), f32),
                pltpu.VMEM((heads, head_size), f32),
                pltpu.VMEM((n_inst // 2, 2 * heads, head_size), bf16),
                pltpu.VMEM((n_inst, 2 * heads, head_size), bf16),
                pltpu.VMEM((n_inst, 2 * heads, head_size), bf16),
                pltpu.VMEM((n_tp, 1, cols), f32),
                pltpu.VMEM((n_tp, 1, cols), f32),
                dma((6,)),
                pltpu.SemaphoreType.REGULAR,
                dma,
                dma,
                dma,
                dma,
                dma,
                dma,
                dma,
                dma,
                dma,
            ],
            compiler_params=pltpu.CompilerParams(
                collective_id=0, has_side_effects=True, vmem_limit_bytes=40 * 1024 * 1024
            ),
            name="paged_decode",
        )(*operands)

    in_specs = (
        P("inst", "tp"),
        P("inst", "tp", None, None),
        P("inst", "tp", None, None),
        P(),
        P(),
        P("tp", None),
    )
    return jax.shard_map(
        body, mesh=mesh, in_specs=in_specs, out_specs=P("inst", "tp"), check_vma=False
    )
```
